512 devices in a mesh: dp: 4 (over x), tensor: 32 (over z_lo, y, core), section: 4 (over z_hi).
Axes of the slice: x: 4, y: 8, z: 8 (z_hi: 4, z_lo: 2; z = z_hi * 2 + z_lo), core: 2. Of those that a mesh axis runs over, the one named last changes fastest.
Arguments:
- partials: bfloat16 [32, 256, 16384], P('tensor', 'dp', 'section'), may hold values from -3 to 3
- residual: bfloat16 [256, 16384], P('dp', 'section'), may hold values from -300 to 300
- norm_gain: bfloat16 [16384], P('section'), may hold values from 0.5 to 1.5
- head_weight: bfloat16 [16384, 65536], P(('section', 'dp'), 'tensor'), may hold values from -0.234375 to 0.234375
- draft_logits: bfloat16 [4, 4, 32, 4, 8192], P('dp', 'section', 'tensor'), may hold values from -300 to 300
- draft_tokens: int32 [64, 4], P(('dp', 'section')), may hold values from 0 to 65535
- live_drafts: int32 [64], P(('dp', 'section')), may hold values from 1 to 4
Outputs:
- residual_rows: float32 [256, 65536], P(('dp', 'section'), 'tensor')
- accept_log: float32 [64, 4], P(('dp', 'section'))
The draws below stay inside these ranges and needn't reach their ends.
All inputs are finite; a program needn't handle non-finite values.
Results may differ from the reference program's by a relative error of at most 0.0082.
Values may be sent and summed in bfloat16 or wider, within the bound.
No kernel may reach another device: no remote copies, remote signals or barrier semaphores. Data moves between devices by JAX's collectives and lax.ppermute only.
A program may use at most 64 MiB of HBM per device.

```python
import math
import jax
import jax.numpy as jnp
import numpy as np
from jax import lax

D = 16384
VT = 2048
K = 4
DOWN = 8
REP = 4
QROWS = 4
R_ALL = 256
SEQS = 64
VOCAB = 65536
VDRAFT = 8192
N_DP = 4
N_TENSOR = 32
N_SECTION = 4


def draw_residual(key, part):
    key = jax.random.fold_in(key, 1)
    key_base, key_row, key_col = jax.random.split(key, 3)
    column = jnp.arange(D, dtype=jnp.float32)[None, :]
    row_scale = jnp.exp(jax.random.uniform(key_row, (R_ALL, 1), jnp.float32, math.log(0.2), math.log(1.5)))
    col_scale = jnp.exp(jax.random.uniform(key_col, (1, D), jnp.float32, math.log(0.2), math.log(1.5)))
    base_draw = jax.random.truncated_normal(key_base, -4.0, 4.0, (R_ALL, D), jnp.float32)
    rising = 1.0 + 2.0 * column / D
    values = base_draw * row_scale * col_scale * rising
    return values.astype(jnp.bfloat16)


def draw_head_weight(key, part):
    key = jax.random.fold_in(key, 2)
    key_base, key_col = jax.random.split(key, 2)
    column = jnp.arange(VOCAB, dtype=jnp.float32)[None, :]
    col_scale = jnp.exp(jax.random.uniform(key_col, (1, VOCAB), jnp.float32, math.log(1.0), math.log(2.5)))
    base_draw = jax.random.truncated_normal(key_base, -4.0, 4.0, (D, VOCAB), jnp.float32)
    rising = 1.0 + 0.15 * column / VOCAB
    values = base_draw * col_scale * rising / math.sqrt(D)
    return values.astype(jnp.bfloat16)


def draw_draft_logits(key, part):
    key = jax.random.fold_in(key, 3)
    key_base, key_col = jax.random.split(key, 2)
    shape = (N_DP, N_SECTION, N_TENSOR, QROWS, VDRAFT)
    owner = jax.lax.broadcasted_iota(jnp.int32, shape, 2)
    entry = jax.lax.broadcasted_iota(jnp.int32, shape, 4)
    col_index = owner // REP * VDRAFT + entry
    col_table = jnp.exp(jax.random.uniform(key_col, (VOCAB,), jnp.float32, math.log(1.0), math.log(2.5)))
    col_scale = col_table[col_index]
    column = col_index.astype(jnp.float32)
    base_draw = jax.random.truncated_normal(key_base, -4.0, 4.0, shape, jnp.float32)
    rising = 1.0 + 0.15 * column / VOCAB
    values = base_draw * col_scale * rising
    return values.astype(jnp.bfloat16)


def touch_ends(values, stream_key, least, top_value):
    longest = values.shape.index(max(values.shape))
    spots = []
    for shift in (0, 1):
        where = [jax.random.randint(jax.random.fold_in(stream_key, axis), (), 0, length) for axis, length in enumerate(values.shape)]
        where[longest] = (where[longest] + shift) % values.shape[longest]
        spots.append(tuple(where))
    return values.at[spots[0]].set(least).at[spots[1]].set(top_value)


def strengthened(values, rng, source, target, blocks, factor):
    def block_of(axis_at):
        return (jnp.arange(values.shape[axis_at]) // (values.shape[axis_at] // blocks)).reshape((-1,) + (1,) * (values.ndim - 1 - axis_at))

    one_side = jax.random.permutation(rng, blocks)[block_of(target)]
    far = (block_of(target) + blocks // 2) % blocks
    return jnp.where((block_of(source) == one_side) | (block_of(source) == far), factor * values, values)


def levels(rng, dims, cuts, least, top_value):
    def one(axis_at, blocks):
        steps = jax.random.uniform(jax.random.fold_in(jax.random.fold_in(rng, 6), axis_at), (blocks,), jnp.float32, least / len(cuts), top_value / len(cuts))
        return jnp.repeat(jnp.exp(steps), dims[axis_at] // blocks).reshape((-1,) + (1,) * (len(dims) - axis_at - 1))

    gain = one(*cuts[0])
    for cut in cuts[1:]:
        gain = gain * one(*cut)
    return gain


def rank_bounds(count, lean):
    loads = [(1 << 20) // math.isqrt(standing ** lean) + 1 for standing in range(1, count + 1)]
    spread = 1 + sum(loads) // (1 << 30)
    return np.cumsum(np.array([max(1, weight // spread) for weight in loads]))


def skewed_ids(rng, extent, count, skew):
    grid = rank_bounds(count, skew)
    lot = jax.random.randint(jax.random.fold_in(rng, 1), extent, 0, int(grid[count - 1]))
    standing = jnp.searchsorted(jnp.asarray(grid, jnp.int32), lot, side="right")
    return jax.random.permutation(jax.random.fold_in(rng, 2), count)[standing].astype(jnp.int32)


def gaussian_with(stream_key, extent, width, bound, pieces, heavy, held_as=jnp.bfloat16):
    entries = width * jax.random.normal(stream_key, extent, jnp.float32)
    if pieces:
        entries = entries * levels(stream_key, extent, pieces, -0.22, 0.18)
    return jnp.clip(strengthened(entries, jax.random.fold_in(stream_key, 3), *heavy), -bound, bound).astype(held_as)


def setup_inputs(seed: int = 0) -> dict:
    key_of = jax.random.split(jax.random.key(seed), 8)
    partials = gaussian_with(key_of[0], (N_TENSOR, R_ALL, D), 0.5, 3.0, ((0, 32), (1, 4), (2, 4)), (0, 2, 32, 2.75))
    residual = draw_residual(jax.random.fold_in(key_of[7], 71), 0)
    norm_gain = jnp.clip(1.0 + 0.1 * jax.random.normal(key_of[2], (D,), jnp.float32), 0.5, 1.5).astype(jnp.bfloat16)
    head_weight = draw_head_weight(jax.random.fold_in(key_of[7], 71), 0)
    draft_logits = draw_draft_logits(jax.random.fold_in(key_of[7], 71), 0)
    draft_tokens = touch_ends(skewed_ids(key_of[5], (SEQS, K), VOCAB, 2), jax.random.fold_in(key_of[5], 3), 0, VOCAB - 1).astype(jnp.int32)
    live_drafts = touch_ends(jax.random.randint(key_of[6], (SEQS,), 1, K + 1), jax.random.fold_in(key_of[6], 1), 1, K).astype(jnp.int32)
    return {"partials": partials, "residual": residual, "norm_gain": norm_gain, "head_weight": head_weight, "draft_logits": draft_logits, "draft_tokens": draft_tokens, "live_drafts": live_drafts}


norm_epsilon = 1e-05

def normalize(values):
    row_peak = lax.optimization_barrier(jnp.max(values, axis=1, keepdims=True))
    exponent = jnp.exp(values - row_peak)
    row_total = lax.optimization_barrier(jnp.sum(exponent, axis=1, keepdims=True))
    return (exponent / row_total, row_peak[:, 0], row_total[:, 0])

def reference(partials, residual, norm_gain, head_weight, draft_logits, draft_tokens, live_drafts):
    layer_total = lax.optimization_barrier(jnp.sum(partials.astype(jnp.float32), axis=0))
    hidden = lax.optimization_barrier((residual.astype(jnp.float32) + layer_total).astype(jnp.bfloat16))
    widened = hidden.astype(jnp.float32)
    mean_square = lax.optimization_barrier(jnp.mean(widened * widened, axis=1, keepdims=True))
    normed = (widened * lax.rsqrt(mean_square + norm_epsilon) * norm_gain.astype(jnp.float32)).astype(jnp.bfloat16)

    def owner_block(owner):
        columns = lax.dynamic_slice_in_dim(head_weight, owner * VT, VT, 1)
        return jnp.dot(normed, columns, preferred_element_type=jnp.float32)
    blocks = lax.map(owner_block, jnp.arange(N_TENSOR, dtype=jnp.int32))
    logits = jnp.transpose(blocks, (1, 0, 2)).reshape(R_ALL, VOCAB)
    drafted = draft_logits.reshape(N_DP, N_SECTION, DOWN, REP, QROWS, VDRAFT)
    drafted = jnp.transpose(drafted, (0, 1, 3, 4, 2, 5)).reshape(R_ALL, VOCAB).astype(jnp.float32)
    target_probs, peak_target, total_target = normalize(logits)
    draft_probs, peak_draft, total_draft = normalize(drafted)
    excess = jnp.maximum(target_probs - draft_probs, 0.0)
    excess_mass = lax.optimization_barrier(jnp.sum(excess, axis=1, keepdims=True))
    position = jnp.arange(R_ALL, dtype=jnp.int32) % K
    live_mask = position < jnp.repeat(live_drafts, K)
    residual_rows = jnp.where(live_mask[:, None], VOCAB * excess / (excess_mass + 1e-06), 0.0)
    tokens = draft_tokens.reshape(R_ALL)
    chosen = jnp.arange(VOCAB, dtype=jnp.int32)[None, :] == tokens[:, None]
    picked_target = lax.optimization_barrier(jnp.sum(jnp.where(chosen, logits, 0.0), axis=1))
    picked_draft = lax.optimization_barrier(jnp.sum(jnp.where(chosen, drafted, 0.0), axis=1))
    log_ratio = picked_target - peak_target - jnp.log(total_target) - (picked_draft - peak_draft - jnp.log(total_draft))
    log_steps = jnp.where(live_mask, jnp.minimum(log_ratio, 0.0), 0.0).reshape(SEQS, K)
    accept_log = jnp.where(live_mask.reshape(SEQS, K), jnp.cumsum(log_steps, axis=1), 0.0)
    return (residual_rows, accept_log)
```

```python
import jax
import jax.numpy as jnp
from jax import lax
from jax.sharding import PartitionSpec as P

norm_epsilon = 1e-05
f32 = jnp.float32
bf16 = jnp.bfloat16
f16 = jnp.float16


def exchange(blocks, axis):
    return lax.all_to_all(blocks, axis, split_axis=0, concat_axis=0, tiled=True)


def share(block, axis):
    copies = lax.axis_size(axis)
    return exchange(jnp.broadcast_to(block[None], (copies,) + block.shape), axis)


def per_device(partials, residual, norm_gain, head_weight, draft_logits, draft_tokens, live_drafts):
    dps = lax.axis_size("dp")
    sections = lax.axis_size("section")
    owners = lax.axis_size("tensor")
    tensor_at = lax.axis_index("tensor")
    rows, width = residual.shape
    feature_count = width * sections
    own_rows = rows // owners
    depth, vocab_slice = head_weight.shape
    seq_count, draft_span = draft_tokens.shape
    row_count = seq_count * draft_span

    draft_block = draft_logits[0, 0, 0]
    source_rows, draft_width = draft_block.shape
    group_size = draft_width // vocab_slice
    groups = [list(range(g, g + group_size)) for g in range(0, owners, group_size)]
    draft_pieces = jnp.transpose(
        draft_block.reshape(source_rows, group_size, vocab_slice), (1, 0, 2)
    )

    terms = exchange(partials[0].reshape(owners, own_rows, width), "tensor")
    layer_total = jnp.sum(terms.astype(f32), axis=0)
    own_residual = lax.dynamic_slice_in_dim(residual, tensor_at * own_rows, own_rows, 0)

    hidden_wide = lax.reduce_precision(own_residual.astype(f32) + layer_total, 8, 7)
    squares_own = jnp.sum(hidden_wide * hidden_wide, axis=1)
    squares_block = jnp.pad(squares_own[:, None], ((0, 8 - own_rows), (0, 127)))
    squares = jnp.sum(share(squares_block, "section").reshape(sections, 8, 128), axis=0)
    factor = lax.rsqrt(squares[:own_rows, :1] / feature_count + norm_epsilon)
    normed_own = (hidden_wide * factor * norm_gain.astype(f32)[None, :]).astype(bf16)

    by_block = jnp.transpose(normed_own.reshape(own_rows, dps, depth), (1, 0, 2))
    to_send = jnp.broadcast_to(by_block[:, None], (dps, owners, own_rows, depth))
    normed = exchange(to_send.reshape(dps * owners, own_rows, depth), ("dp", "tensor"))
    normed = normed.reshape(dps * rows, depth)
    products = jnp.dot(normed, head_weight, preferred_element_type=f32).astype(f16)

    gathered = exchange(products, ("dp", "section"))
    gathered = gathered.reshape(dps * sections, row_count, vocab_slice)
    logits = jnp.sum(gathered.astype(f32), axis=0)

    drafted = lax.all_to_all(
        draft_pieces, "tensor", 0, 0, axis_index_groups=groups, tiled=True
    ).reshape(row_count, vocab_slice).astype(f32)

    tokens_flat = draft_tokens.reshape(row_count)
    local_ids = tokens_flat - tensor_at * vocab_slice
    chosen = lax.broadcasted_iota(jnp.int32, (row_count, vocab_slice), 1) == local_ids[:, None]

    def statistics(values):
        peak = jnp.max(values, axis=1)
        exps = jnp.exp(values - peak[:, None])
        pick = jnp.sum(jnp.where(chosen, values, 0.0), axis=1)
        return exps, [peak, jnp.sum(exps, axis=1), pick]

    exp_draft, stats_draft = statistics(drafted)
    exp_target, stats_target = statistics(logits)
    stats = jnp.stack(stats_target + stats_draft + [stats_target[0]] * 2)
    stats = jnp.pad(stats, ((0, 0), (0, 128 - row_count)))
    stats = share(stats, "tensor").reshape(owners, 8, 128)[:, :, :row_count]

    def combine(peaks, totals, picks, own_peak):
        peak = jnp.max(peaks, axis=0)
        total = jnp.sum(totals * jnp.exp(peaks - peak[None]), axis=0)
        return peak, total, jnp.sum(picks, axis=0), jnp.exp(own_peak - peak) / total

    peak_target, total_target, pick_target, scale_target = combine(
        stats[:, 0], stats[:, 1], stats[:, 2], stats_target[0]
    )
    peak_draft, total_draft, pick_draft, scale_draft = combine(
        stats[:, 3], stats[:, 4], stats[:, 5], stats_draft[0]
    )
    excess = jnp.maximum(
        exp_target * scale_target[:, None] - exp_draft * scale_draft[:, None], 0.0
    )
    mass = jnp.pad(jnp.sum(excess, axis=1), (0, 128 - row_count))
    mass = share(jnp.broadcast_to(mass[None], (8, 128)), "tensor").reshape(owners, 8, 128)
    excess_mass = jnp.sum(mass[:, 0, :row_count], axis=0)

    vocab_total = vocab_slice * owners
    position = lax.broadcasted_iota(jnp.int32, (row_count,), 0) % draft_span
    live_mask = position < jnp.repeat(live_drafts, draft_span)
    row_scale = jnp.where(live_mask, vocab_total / (excess_mass + 1e-06), 0.0)
    residual_rows = excess * row_scale[:, None]
    log_ratio = (
        pick_target
        - peak_target
        - jnp.log(total_target)
        - (pick_draft - peak_draft - jnp.log(total_draft))
    )
    log_steps = jnp.where(live_mask, jnp.minimum(log_ratio, 0.0), 0.0).reshape(
        seq_count, draft_span
    )
    accept_log = jnp.where(
        live_mask.reshape(seq_count, draft_span), jnp.cumsum(log_steps, axis=1), 0.0
    )
    return (residual_rows, accept_log)


def solution(mesh):
    return jax.shard_map(
        per_device,
        mesh=mesh,
        in_specs=(
            P("tensor", "dp", "section"),
            P("dp", "section"),
            P("section"),
            P(("section", "dp"), "tensor"),
            P("dp", "section", "tensor", None, None),
            P(("dp", "section"), None),
            P(("dp", "section")),
        ),
        out_specs=(P(("dp", "section"), "tensor"), P(("dp", "section"), None)),
        check_vma=False,
    )
```

```python
import jax
import jax.numpy as jnp
from jax import lax
from jax.experimental import pallas as pl
from jax.experimental.pallas import tpu as pltpu
from jax.sharding import Mesh, PartitionSpec as P

norm_epsilon = 1e-05
f32 = jnp.float32
bf16 = jnp.bfloat16
f16 = jnp.float16
tensor_axes = ("zy", "core")


def exchange(blocks, axis):
    return lax.all_to_all(blocks, axis, split_axis=0, concat_axis=0, tiled=True)


def share(values):
    copies = lax.axis_size(tensor_axes)
    row = jnp.pad(values[None], ((0, 0), (0, 128 - values.shape[0])))
    return exchange(jnp.broadcast_to(row[None], (copies, 1, 128)), tensor_axes)


def head_kernel(x_ref, w_ref, o_ref):
    o_ref[...] = jnp.dot(x_ref[...], w_ref[...], preferred_element_type=f32)


def head_product(x, w):
    rows, depth = x.shape
    columns = w.shape[1]
    step = min(1024, columns)
    return pl.pallas_call(
        head_kernel,
        grid=(columns // step,),
        in_specs=[
            pl.BlockSpec((rows, depth), lambda i: (0, 0)),
            pl.BlockSpec((depth, step), lambda i: (0, i)),
        ],
        out_specs=pl.BlockSpec((rows, step), lambda i: (0, i)),
        out_shape=jax.ShapeDtypeStruct((rows, columns), f32),
        compiler_params=pltpu.CompilerParams(vmem_limit_bytes=16 << 20),
        name="head_product",
    )(x, w)


def per_device(partials, residual, norm_gain, head_weight, draft_logits, draft_tokens, live_drafts):
    dps = lax.axis_size("dp")
    sections = lax.axis_size("section")
    cores = lax.axis_size("core")
    owners = lax.axis_size(tensor_axes)
    chips = owners // cores
    tensor_at = lax.axis_index(tensor_axes)
    core_at = lax.axis_index("core")
    rows, width = residual.shape
    feature_count = width * sections
    own_rows = rows // owners
    depth, vocab_slice = head_weight.shape
    seq_count, draft_span = draft_tokens.shape
    row_count = seq_count * draft_span

    terms = exchange(partials[0].reshape(owners, own_rows, width), ("core", "zy"))
    layer_total = jnp.sum(terms.astype(f32), axis=0)
    own_at = (core_at * chips + lax.axis_index("zy")) * own_rows
    own_residual = lax.dynamic_slice_in_dim(residual, own_at, own_rows, 0)

    hidden = lax.reduce_precision(own_residual.astype(f32) + layer_total, 8, 7)
    squares = lax.psum(jnp.sum(hidden * hidden, axis=1), "section")
    factor = lax.rsqrt(squares / feature_count + norm_epsilon)
    normed_own = (hidden * factor[:, None] * norm_gain.astype(f32)[None, :]).astype(bf16)

    by_block = jnp.transpose(normed_own.reshape(own_rows, dps, depth), (1, 0, 2))
    to_send = jnp.broadcast_to(by_block[:, None], (dps, chips, own_rows, depth))
    mine = exchange(to_send.reshape(dps * chips, own_rows, depth), ("dp", "zy"))
    mine = mine.reshape(dps, rows // cores, depth)
    other = lax.ppermute(mine, "core", [(0, 1), (1, 0)])
    normed = jnp.where(
        core_at == 0, jnp.stack([mine, other], axis=1), jnp.stack([other, mine], axis=1)
    ).reshape(dps * rows, depth)
    products = head_product(normed, head_weight).astype(f16)

    by_dp = exchange(products, "dp").reshape(dps, rows, vocab_slice)
    by_dp = jnp.sum(by_dp.astype(f32), axis=0).astype(f16)
    gathered = exchange(by_dp, "section").reshape(sections, row_count, vocab_slice)
    logits = jnp.sum(gathered.astype(f32), axis=0)

    draft_block = draft_logits[0, 0, 0]
    source_rows, draft_width = draft_block.shape
    group_size = draft_width // vocab_slice
    member = tensor_at % group_size
    pieces = jnp.transpose(
        draft_block.reshape(source_rows, group_size, vocab_slice), (1, 0, 2)
    )
    arrived = []
    for flip in range(group_size):
        piece = lax.dynamic_index_in_dim(pieces, member ^ flip, 0, keepdims=False)
        if flip:
            piece = lax.ppermute(piece, tensor_axes, [(i, i ^ flip) for i in range(owners)])
        arrived.append(piece)
    arrived = jnp.stack(arrived)
    drafted = jnp.concatenate(
        [
            lax.dynamic_index_in_dim(arrived, member ^ source, 0, keepdims=False)
            for source in range(group_size)
        ]
    ).astype(f32)

    tokens_flat = draft_tokens.reshape(row_count)
    local_ids = tokens_flat - tensor_at * vocab_slice
    chosen = lax.broadcasted_iota(jnp.int32, (row_count, vocab_slice), 1) == local_ids[:, None]

    def statistics(values):
        peak = jnp.max(values, axis=1)
        exps = jnp.exp(values - peak[:, None])
        pick = jnp.sum(jnp.where(chosen, values, 0.0), axis=1)
        return exps, [peak, jnp.sum(exps, axis=1), pick]

    exp_draft, stats_draft = statistics(drafted)
    exp_target, stats_target = statistics(logits)
    stats = share(jnp.concatenate(stats_target + stats_draft))
    stats = stats[:, 0, : 6 * row_count].reshape(owners, 6, row_count)

    def combine(peaks, totals, picks, own_peak):
        peak = jnp.max(peaks, axis=0)
        total = jnp.sum(totals * jnp.exp(peaks - peak[None]), axis=0)
        return peak, total, jnp.sum(picks, axis=0), jnp.exp(own_peak - peak) / total

    peak_target, total_target, pick_target, scale_target = combine(
        stats[:, 0], stats[:, 1], stats[:, 2], stats_target[0]
    )
    peak_draft, total_draft, pick_draft, scale_draft = combine(
        stats[:, 3], stats[:, 4], stats[:, 5], stats_draft[0]
    )
    excess = jnp.maximum(
        exp_target * scale_target[:, None] - exp_draft * scale_draft[:, None], 0.0
    )
    mass = share(jnp.sum(excess, axis=1))
    excess_mass = jnp.sum(mass[:, 0, :row_count], axis=0)

    vocab_total = vocab_slice * owners
    position = lax.broadcasted_iota(jnp.int32, (row_count,), 0) % draft_span
    live_mask = position < jnp.repeat(live_drafts, draft_span)
    row_scale = jnp.where(live_mask, vocab_total / (excess_mass + 1e-06), 0.0)
    residual_rows = excess * row_scale[:, None]
    log_ratio = (
        pick_target
        - peak_target
        - jnp.log(total_target)
        - (pick_draft - peak_draft - jnp.log(total_draft))
    )
    log_steps = jnp.where(live_mask, jnp.minimum(log_ratio, 0.0), 0.0).reshape(
        seq_count, draft_span
    )
    accept_log = jnp.where(
        live_mask.reshape(seq_count, draft_span), jnp.cumsum(log_steps, axis=1), 0.0
    )
    return (residual_rows, accept_log)


def solution(mesh):
    sizes = mesh.shape
    split = Mesh(
        mesh.devices.reshape(sizes["dp"], sizes["tensor"] // 2, 2, sizes["section"]),
        ("dp",) + tensor_axes + ("section",),
    )
    return jax.shard_map(
        per_device,
        mesh=split,
        in_specs=(
            P(tensor_axes, "dp", "section"),
            P("dp", "section"),
            P("section"),
            P(("section", "dp"), tensor_axes),
            P("dp", "section", tensor_axes, None, None),
            P(("dp", "section"), None),
            P(("dp", "section")),
        ),
        out_specs=(P(("dp", "section"), tensor_axes), P(("dp", "section"), None)),
        check_vma=False,
    )
```

```python
import functools

import jax
import jax.numpy as jnp
from jax import lax
from jax.experimental import pallas as pl
from jax.experimental.pallas import tpu as pltpu
from jax.sharding import Mesh, PartitionSpec as P

norm_epsilon = 1e-05
f32 = jnp.float32
bf16 = jnp.bfloat16
f16 = jnp.float16
tensor_axes = ("zy", "core")


def exchange(blocks, axis):
    return lax.all_to_all(blocks, axis, split_axis=0, concat_axis=0, tiled=True)


def one_row(values):
    return jnp.pad(values[None], ((0, 0), (0, 128 - values.shape[0])))


def share(values):
    copies = lax.axis_size(tensor_axes)
    return exchange(jnp.broadcast_to(one_row(values)[None], (copies, 1, 128)), tensor_axes)


def head_kernel(x_ref, top_ref, w_hbm, o_ref, bottom, arrived):
    depth = top_ref.shape[0]
    part = depth // 2
    copies = [
        pltpu.make_async_copy(
            w_hbm.at[pl.ds(depth + i * part, part), :],
            bottom.at[pl.ds(i * part, part), :],
            arrived.at[i],
        )
        for i in range(2)
    ]
    for copy in copies:
        copy.start()
    o_ref[...] = jnp.dot(x_ref[:, :depth], top_ref[...], preferred_element_type=f32)
    for i, copy in enumerate(copies):
        copy.wait()
        o_ref[...] += jnp.dot(
            x_ref[:, depth + i * part : depth + (i + 1) * part],
            bottom[pl.ds(i * part, part), :],
            preferred_element_type=f32,
        )


def head_product(x, top, w):
    rows, columns = x.shape[0], w.shape[1]
    return pl.pallas_call(
        head_kernel,
        in_specs=[
            pl.BlockSpec(memory_space=pltpu.VMEM),
            pl.BlockSpec(memory_space=pltpu.VMEM),
            pl.BlockSpec(memory_space=pl.ANY),
        ],
        out_specs=pl.BlockSpec(memory_space=pltpu.VMEM),
        out_shape=jax.ShapeDtypeStruct((rows, columns), f32),
        scratch_shapes=[pltpu.VMEM(top.shape, w.dtype), pltpu.SemaphoreType.DMA((2,))],
        compiler_params=pltpu.CompilerParams(vmem_limit_bytes=48 << 20),
        name="head_product",
    )(x, top, w)


def finish_kernel(vocab_total, excess_ref, mass_ref, ratio_ref, live_ref, rows_ref, accept_ref):
    row_count = excess_ref.shape[0]
    seq_count, span = accept_ref.shape
    position = lax.broadcasted_iota(jnp.int32, (1, 128), 1) % span
    live = position < live_ref[...]
    excess_mass = jnp.sum(mass_ref[...], axis=0)
    scale = jnp.where(live, vocab_total / (excess_mass + 1e-06), 0.0)
    row = lax.broadcasted_iota(jnp.int32, (row_count, 128), 0)
    lane = lax.broadcasted_iota(jnp.int32, (row_count, 128), 1)
    column = jnp.sum(jnp.where(row == lane, scale, 0.0), axis=1, keepdims=True)
    rows_ref[...] = excess_ref[...] * column
    steps = jnp.where(live, jnp.minimum(ratio_ref[...], 0.0), 0.0)
    row = lax.broadcasted_iota(jnp.int32, (seq_count, 128), 0)
    lane = lax.broadcasted_iota(jnp.int32, (seq_count, 128), 1)
    total = jnp.zeros((seq_count, 1), f32)
    for k in range(span):
        at = lane == row * span + k
        total = total + jnp.sum(jnp.where(at, steps, 0.0), axis=1, keepdims=True)
        alive = jnp.sum(jnp.where(at & live, 1.0, 0.0), axis=1, keepdims=True)
        accept_ref[:, k : k + 1] = jnp.where(alive > 0.0, total, 0.0)


def finish(excess, mass, log_ratio, live_rows, vocab_total, seq_count, span):
    return pl.pallas_call(
        functools.partial(finish_kernel, float(vocab_total)),
        out_shape=(
            jax.ShapeDtypeStruct(excess.shape, f32),
            jax.ShapeDtypeStruct((seq_count, span), f32),
        ),
        compiler_params=pltpu.CompilerParams(vmem_limit_bytes=4 << 20),
        name="finish",
    )(excess, mass, log_ratio, live_rows)


def per_device(partials, residual, norm_gain, head_weight, draft_logits, draft_tokens, live_drafts):
    dps = lax.axis_size("dp")
    sections = lax.axis_size("section")
    cores = lax.axis_size("core")
    owners = lax.axis_size(tensor_axes)
    chips = owners // cores
    tensor_at = lax.axis_index(tensor_axes)
    core_at = lax.axis_index("core")
    rows, width = residual.shape
    feature_count = width * sections
    own_rows = rows // owners
    depth, vocab_slice = head_weight.shape
    seq_count, draft_span = draft_tokens.shape
    row_count = seq_count * draft_span

    draft_block = draft_logits[0, 0, 0]
    source_rows, draft_width = draft_block.shape
    group_size = draft_width // vocab_slice
    member = tensor_at % group_size

    def draft_piece(block, flip):
        return lax.dynamic_slice_in_dim(block, (member ^ flip) * vocab_slice, vocab_slice, 1)

    terms = partials[0]
    half = rows // cores
    kept = lax.dynamic_slice_in_dim(terms, core_at * half, half, 0)
    given = lax.dynamic_slice_in_dim(terms, (1 - core_at) * half, half, 0)
    beside = draft_piece(draft_block, 1)
    beside = jnp.pad(beside, ((0, 8 - source_rows), (0, width - vocab_slice)))
    got = lax.ppermute(
        jnp.concatenate([given, beside]), "core", [(i, cores - 1 - i) for i in range(cores)]
    )
    own_at = (core_at * chips + lax.axis_index("zy")) * own_rows
    own_residual = lax.dynamic_slice_in_dim(residual, own_at, own_rows, 0)
    lanes = width // 8
    own_residual = own_residual.reshape(own_rows, 8, lanes).astype(f32)
    gain = norm_gain.reshape(8, lanes).astype(f32)
    got, kept, own_residual, gain, draft_block, head_weight = lax.optimization_barrier(
        (got, kept, own_residual, gain, draft_block, head_weight)
    )
    arrived = [draft_piece(draft_block, 0), got[half : half + source_rows, :vocab_slice]]
    got = got[:half]
    pair = (kept.astype(f32) + got.astype(f32)).astype(f16)
    pair_sums = exchange(pair.reshape(chips, own_rows, 8, lanes), "zy")
    for flip in range(2, group_size):
        arrived.append(
            lax.ppermute(
                draft_piece(draft_block, flip), tensor_axes, [(i, i ^ flip) for i in range(owners)]
            )
        )
    arrived = jnp.stack(arrived)
    pair_sums, weight_top = lax.optimization_barrier((pair_sums, head_weight[: depth // 2]))
    layer_total = jnp.sum(pair_sums.astype(f32), axis=0)

    hidden = lax.reduce_precision(own_residual + layer_total, 8, 7)
    squares = lax.psum(jnp.sum(hidden * hidden, axis=(1, 2)), "section")
    factor = lax.rsqrt(squares / feature_count + norm_epsilon)
    normed_own = (hidden * factor[:, None, None] * gain[None]).astype(bf16)

    normed_own, arrived, draft_tokens, live_drafts, core_at, tensor_at, member = (
        lax.optimization_barrier(
            (normed_own, arrived, draft_tokens, live_drafts, core_at, tensor_at, member)
        )
    )

    by_block = jnp.transpose(normed_own.reshape(own_rows, dps, depth), (1, 0, 2))
    to_send = jnp.broadcast_to(by_block[:, None], (dps, chips, own_rows, depth))
    mine = exchange(to_send.reshape(dps * chips, own_rows, depth), ("dp", "zy"))
    mine = mine.reshape(dps, rows // cores, depth)
    mine, arrived, draft_tokens, live_drafts, core_at, tensor_at, member = (
        lax.optimization_barrier(
            (mine, arrived, draft_tokens, live_drafts, core_at, tensor_at, member)
        )
    )
    other = lax.ppermute(mine, "core", [(0, 1), (1, 0)])

    drafted = jnp.concatenate(
        [
            lax.dynamic_index_in_dim(arrived, member ^ source, 0, keepdims=False)
            for source in range(group_size)
        ]
    ).astype(f32)
    local_ids = draft_tokens.reshape(row_count) - tensor_at * vocab_slice
    live_rows = one_row(jnp.repeat(live_drafts, draft_span))

    def statistics(values):
        peak = jnp.max(values, axis=1)
        exps = jnp.exp(values - peak[:, None])
        chosen = lax.broadcasted_iota(jnp.int32, values.shape, 1) == local_ids[:, None]
        pick = jnp.sum(jnp.where(chosen, values, 0.0), axis=1)
        return exps, [peak, jnp.sum(exps, axis=1), pick]

    exp_draft, stats_draft = statistics(drafted)
    other, exp_draft, stats_draft, live_rows, local_ids = lax.optimization_barrier(
        (other, exp_draft, stats_draft, live_rows, local_ids)
    )

    normed = jnp.where(
        core_at == 0, jnp.stack([mine, other], axis=1), jnp.stack([other, mine], axis=1)
    ).reshape(dps * rows, depth)
    products = head_product(normed, weight_top, head_weight)
    products = products.astype(f16)

    by_dp = exchange(products, "dp").reshape(dps, rows, vocab_slice)

    by_dp = jnp.sum(by_dp.astype(f32), axis=0).astype(f16)
    gathered = exchange(by_dp, "section").reshape(sections, row_count, vocab_slice)
    logits = jnp.sum(gathered.astype(f32), axis=0)

    exp_target, stats_target = statistics(logits)
    stats = share(jnp.concatenate(stats_target + stats_draft))
    stats = stats[:, 0, : 6 * row_count].reshape(owners, 6, row_count)

    def combine(peaks, totals, picks, own_peak):
        peak = jnp.max(peaks, axis=0)
        total = jnp.sum(totals * jnp.exp(peaks - peak[None]), axis=0)
        return peak, total, jnp.sum(picks, axis=0), jnp.exp(own_peak - peak) / total

    peak_target, total_target, pick_target, scale_target = combine(
        stats[:, 0], stats[:, 1], stats[:, 2], stats_target[0]
    )
    peak_draft, total_draft, pick_draft, scale_draft = combine(
        stats[:, 3], stats[:, 4], stats[:, 5], stats_draft[0]
    )
    excess = jnp.maximum(
        exp_target * scale_target[:, None] - exp_draft * scale_draft[:, None], 0.0
    )
    log_ratio = (
        pick_target
        - peak_target
        - jnp.log(total_target)
        - (pick_draft - peak_draft - jnp.log(total_draft))
    )
    excess, log_ratio, live_rows = lax.optimization_barrier(
        (excess, one_row(log_ratio), live_rows)
    )
    mass = share(jnp.sum(excess, axis=1))
    return finish(
        excess, mass, log_ratio, live_rows, vocab_slice * owners, seq_count, draft_span
    )


def solution(mesh):
    sizes = mesh.shape
    split = Mesh(
        mesh.devices.reshape(sizes["dp"], sizes["tensor"] // 2, 2, sizes["section"]),
        ("dp",) + tensor_axes + ("section",),
    )
    return jax.shard_map(
        per_device,
        mesh=split,
        in_specs=(
            P(tensor_axes, "dp", "section"),
            P("dp", "section"),
            P("section"),
            P(("section", "dp"), tensor_axes),
            P("dp", "section", tensor_axes, None, None),
            P(("dp", "section"), None),
            P(("dp", "section")),
        ),
        out_specs=(P(("dp", "section"), tensor_axes), P(("dp", "section"), None)),
        check_vma=False,
    )
```

```python
import functools

import jax
import jax.numpy as jnp
from jax import lax
from jax.experimental import pallas as pl
from jax.experimental.pallas import tpu as pltpu
from jax.sharding import Mesh, PartitionSpec as P

norm_epsilon = 1e-05
f32 = jnp.float32
bf16 = jnp.bfloat16
f16 = jnp.float16
pair_scale = 8192.0
block_scale = 32.0
dp_scale = 16.0
tensor_axes = ("zy", "core")


def exchange(blocks, axis):
    return lax.all_to_all(blocks, axis, split_axis=0, concat_axis=0, tiled=True)


def one_row(values):
    return jnp.pad(values[None], ((0, 0), (0, 128 - values.shape[0])))


def share(values):
    copies = lax.axis_size(tensor_axes)
    return exchange(jnp.broadcast_to(one_row(values)[None], (copies, 1, 128)), tensor_axes)


def head_kernel(x_ref, top_ref, w_hbm, o_ref, bottom, arrived):
    depth = top_ref.shape[0]
    part = depth // 2
    copies = [
        pltpu.make_async_copy(
            w_hbm.at[pl.ds(depth + i * part, part), :],
            bottom.at[pl.ds(i * part, part), :],
            arrived.at[i],
        )
        for i in range(2)
    ]
    for copy in copies:
        copy.start()
    o_ref[...] = jnp.dot(x_ref[:, :depth], top_ref[...], preferred_element_type=f32)
    for i, copy in enumerate(copies):
        copy.wait()
        o_ref[...] += jnp.dot(
            x_ref[:, depth + i * part : depth + (i + 1) * part],
            bottom[pl.ds(i * part, part), :],
            preferred_element_type=f32,
        )


def head_product(x, top, w):
    rows, columns = x.shape[0], w.shape[1]
    return pl.pallas_call(
        head_kernel,
        in_specs=[
            pl.BlockSpec(memory_space=pltpu.VMEM),
            pl.BlockSpec(memory_space=pltpu.VMEM),
            pl.BlockSpec(memory_space=pl.ANY),
        ],
        out_specs=pl.BlockSpec(memory_space=pltpu.VMEM),
        out_shape=jax.ShapeDtypeStruct((rows, columns), f32),
        scratch_shapes=[pltpu.VMEM(top.shape, w.dtype), pltpu.SemaphoreType.DMA((2,))],
        compiler_params=pltpu.CompilerParams(vmem_limit_bytes=48 << 20),
        name="head_product",
    )(x, top, w)


def finish_kernel(vocab_total, excess_ref, mass_ref, ratio_ref, live_ref, rows_ref, accept_ref):
    row_count = excess_ref.shape[0]
    seq_count, span = accept_ref.shape
    position = lax.broadcasted_iota(jnp.int32, (1, 128), 1) % span
    live = position < live_ref[...]
    excess_mass = jnp.sum(mass_ref[...], axis=0)
    scale = jnp.where(live, vocab_total / (excess_mass + 1e-06), 0.0)
    row = lax.broadcasted_iota(jnp.int32, (row_count, 128), 0)
    lane = lax.broadcasted_iota(jnp.int32, (row_count, 128), 1)
    column = jnp.sum(jnp.where(row == lane, scale, 0.0), axis=1, keepdims=True)
    rows_ref[...] = excess_ref[...] * column
    steps = jnp.where(live, jnp.minimum(ratio_ref[...], 0.0), 0.0)
    row = lax.broadcasted_iota(jnp.int32, (seq_count, 128), 0)
    lane = lax.broadcasted_iota(jnp.int32, (seq_count, 128), 1)
    total = jnp.zeros((seq_count, 1), f32)
    for k in range(span):
        at = lane == row * span + k
        total = total + jnp.sum(jnp.where(at, steps, 0.0), axis=1, keepdims=True)
        alive = jnp.sum(jnp.where(at & live, 1.0, 0.0), axis=1, keepdims=True)
        accept_ref[:, k : k + 1] = jnp.where(alive > 0.0, total, 0.0)


def finish(excess, mass, log_ratio, live_rows, vocab_total, seq_count, span):
    return pl.pallas_call(
        functools.partial(finish_kernel, float(vocab_total)),
        out_shape=(
            jax.ShapeDtypeStruct(excess.shape, f32),
            jax.ShapeDtypeStruct((seq_count, span), f32),
        ),
        compiler_params=pltpu.CompilerParams(vmem_limit_bytes=4 << 20),
        name="finish",
    )(excess, mass, log_ratio, live_rows)


def per_device(partials, residual, norm_gain, head_weight, draft_logits, draft_tokens, live_drafts):
    dps = lax.axis_size("dp")
    sections = lax.axis_size("section")
    cores = lax.axis_size("core")
    owners = lax.axis_size(tensor_axes)
    chips = owners // cores
    tensor_at = lax.axis_index(tensor_axes)
    core_at = lax.axis_index("core")
    rows, width = residual.shape
    feature_count = width * sections
    own_rows = rows // owners
    depth, vocab_slice = head_weight.shape
    seq_count, draft_span = draft_tokens.shape
    row_count = seq_count * draft_span

    draft_block = draft_logits[0, 0, 0]
    source_rows, draft_width = draft_block.shape
    group_size = draft_width // vocab_slice
    member = tensor_at % group_size

    def draft_piece(block, flip):
        return lax.dynamic_slice_in_dim(block, (member ^ flip) * vocab_slice, vocab_slice, 1)

    terms = partials[0]
    half = rows // cores
    kept = lax.dynamic_slice_in_dim(terms, core_at * half, half, 0)
    given = lax.dynamic_slice_in_dim(terms, (1 - core_at) * half, half, 0)
    beside = draft_piece(draft_block, 1)
    beside = jnp.pad(beside, ((0, 8 - source_rows), (0, width - vocab_slice)))
    got = lax.ppermute(
        jnp.concatenate([given, beside]), "core", [(i, cores - 1 - i) for i in range(cores)]
    )
    own_at = (core_at * chips + lax.axis_index("zy")) * own_rows
    own_residual = lax.dynamic_slice_in_dim(residual, own_at, own_rows, 0)
    lanes = width // 8
    own_residual = own_residual.reshape(own_rows, 8, lanes).astype(f32)
    gain = norm_gain.reshape(8, lanes).astype(f32)
    got, kept, own_residual, gain, draft_block, head_weight = lax.optimization_barrier(
        (got, kept, own_residual, gain, draft_block, head_weight)
    )
    arrived = [draft_piece(draft_block, 0), got[half : half + source_rows, :vocab_slice]]
    got = got[:half]
    pair = ((kept.astype(f32) + got.astype(f32)) * pair_scale).astype(f16)
    pair_sums = exchange(pair.reshape(chips, own_rows, 8, lanes), "zy")
    for flip in range(2, group_size):
        arrived.append(
            lax.ppermute(
                draft_piece(draft_block, flip), tensor_axes, [(i, i ^ flip) for i in range(owners)]
            )
        )
    arrived = jnp.stack(arrived)
    pair_sums, weight_top = lax.optimization_barrier((pair_sums, head_weight[: depth // 2]))
    layer_total = jnp.sum(pair_sums.astype(f32), axis=0) * (1.0 / pair_scale)

    hidden = lax.reduce_precision(own_residual + layer_total, 8, 7)
    squares = lax.psum(jnp.sum(hidden * hidden, axis=(1, 2)), "section")
    factor = lax.rsqrt(squares / feature_count + norm_epsilon)
    normed_own = (hidden * factor[:, None, None] * gain[None]).astype(bf16)

    normed_own, arrived, draft_tokens, live_drafts, core_at, tensor_at, member = (
        lax.optimization_barrier(
            (normed_own, arrived, draft_tokens, live_drafts, core_at, tensor_at, member)
        )
    )

    by_block = jnp.transpose(normed_own.reshape(own_rows, dps, depth), (1, 0, 2))
    to_send = jnp.broadcast_to(by_block[:, None], (dps, chips, own_rows, depth))
    mine = exchange(to_send.reshape(dps * chips, own_rows, depth), ("dp", "zy"))
    mine = mine.reshape(dps, rows // cores, depth)
    mine, arrived, draft_tokens, live_drafts, core_at, tensor_at, member = (
        lax.optimization_barrier(
            (mine, arrived, draft_tokens, live_drafts, core_at, tensor_at, member)
        )
    )
    other = lax.ppermute(mine, "core", [(0, 1), (1, 0)])

    drafted = jnp.concatenate(
        [
            lax.dynamic_index_in_dim(arrived, member ^ source, 0, keepdims=False)
            for source in range(group_size)
        ]
    ).astype(f32)
    local_ids = draft_tokens.reshape(row_count) - tensor_at * vocab_slice
    live_rows = one_row(jnp.repeat(live_drafts, draft_span))

    def statistics(values):
        peak = jnp.max(values, axis=1)
        exps = jnp.exp(values - peak[:, None])
        chosen = lax.broadcasted_iota(jnp.int32, values.shape, 1) == local_ids[:, None]
        pick = jnp.sum(jnp.where(chosen, values, 0.0), axis=1)
        return exps, [peak, jnp.sum(exps, axis=1), pick]

    exp_draft, stats_draft = statistics(drafted)
    other, exp_draft, stats_draft, live_rows, local_ids = lax.optimization_barrier(
        (other, exp_draft, stats_draft, live_rows, local_ids)
    )

    normed = jnp.where(
        core_at == 0, jnp.stack([mine, other], axis=1), jnp.stack([other, mine], axis=1)
    ).reshape(dps * rows, depth)
    products = head_product(normed, weight_top, head_weight)
    products = (products * block_scale).astype(f16)

    by_dp = exchange(products, "dp").reshape(dps, rows, vocab_slice)

    by_dp = (jnp.sum(by_dp.astype(f32), axis=0) * (dp_scale / block_scale)).astype(f16)
    gathered = exchange(by_dp, "section").reshape(sections, row_count, vocab_slice)
    logits = jnp.sum(gathered.astype(f32), axis=0) * (1.0 / dp_scale)

    exp_target, stats_target = statistics(logits)
    stats = share(jnp.concatenate(stats_target + stats_draft))
    stats = stats[:, 0, : 6 * row_count].reshape(owners, 6, row_count)

    def combine(peaks, totals, picks, own_peak):
        peak = jnp.max(peaks, axis=0)
        total = jnp.sum(totals * jnp.exp(peaks - peak[None]), axis=0)
        return peak, total, jnp.sum(picks, axis=0), jnp.exp(own_peak - peak) / total

    peak_target, total_target, pick_target, scale_target = combine(
        stats[:, 0], stats[:, 1], stats[:, 2], stats_target[0]
    )
    peak_draft, total_draft, pick_draft, scale_draft = combine(
        stats[:, 3], stats[:, 4], stats[:, 5], stats_draft[0]
    )
    excess = jnp.maximum(
        exp_target * scale_target[:, None] - exp_draft * scale_draft[:, None], 0.0
    )
    log_ratio = (
        pick_target
        - peak_target
        - jnp.log(total_target)
        - (pick_draft - peak_draft - jnp.log(total_draft))
    )
    excess, log_ratio, live_rows = lax.optimization_barrier(
        (excess, one_row(log_ratio), live_rows)
    )
    mass = share(jnp.sum(excess, axis=1))
    return finish(
        excess, mass, log_ratio, live_rows, vocab_slice * owners, seq_count, draft_span
    )


def solution(mesh):
    sizes = mesh.shape
    split = Mesh(
        mesh.devices.reshape(sizes["dp"], sizes["tensor"] // 2, 2, sizes["section"]),
        ("dp",) + tensor_axes + ("section",),
    )
    return jax.shard_map(
        per_device,
        mesh=split,
        in_specs=(
            P(tensor_axes, "dp", "section"),
            P("dp", "section"),
            P("section"),
            P(("section", "dp"), tensor_axes),
            P("dp", "section", tensor_axes, None, None),
            P(("dp", "section"), None),
            P(("dp", "section")),
        ),
        out_specs=(P(("dp", "section"), tensor_axes), P(("dp", "section"), None)),
        check_vma=False,
    )
```

```python
import functools

import jax
import jax.numpy as jnp
from jax import lax
from jax.experimental import pallas as pl
from jax.experimental.pallas import tpu as pltpu
from jax.sharding import Mesh, PartitionSpec as P

norm_epsilon = 1e-05
f32 = jnp.float32
bf16 = jnp.bfloat16
f16 = jnp.float16
pair_scale = 8192.0
block_scale = 32.0
dp_scale = 16.0
tensor_axes = ("zy", "core")


def exchange(blocks, axis):
    return lax.all_to_all(blocks, axis, split_axis=0, concat_axis=0, tiled=True)


share_axes = tensor_axes[::-1]


def one_row(values):
    return jnp.pad(values[None], ((0, 0), (0, 128 - values.shape[0])))


def head_kernel(x_ref, top_ref, w_hbm, o_ref, bottom, arrived):
    depth = top_ref.shape[0]
    part = depth // 2
    copies = [
        pltpu.make_async_copy(
            w_hbm.at[pl.ds(depth + i * part, part), :],
            bottom.at[pl.ds(i * part, part), :],
            arrived.at[i],
        )
        for i in range(2)
    ]
    for copy in copies:
        copy.start()
    o_ref[...] = jnp.dot(x_ref[:, :depth], top_ref[...], preferred_element_type=f32)
    for i, copy in enumerate(copies):
        copy.wait()
        o_ref[...] += jnp.dot(
            x_ref[:, depth + i * part : depth + (i + 1) * part],
            bottom[pl.ds(i * part, part), :],
            preferred_element_type=f32,
        )


def head_product(x, top, w):
    rows, columns = x.shape[0], w.shape[1]
    return pl.pallas_call(
        head_kernel,
        in_specs=[
            pl.BlockSpec(memory_space=pltpu.VMEM),
            pl.BlockSpec(memory_space=pltpu.VMEM),
            pl.BlockSpec(memory_space=pl.ANY),
        ],
        out_specs=pl.BlockSpec(memory_space=pltpu.VMEM),
        out_shape=jax.ShapeDtypeStruct((rows, columns), f32),
        scratch_shapes=[pltpu.VMEM(top.shape, w.dtype), pltpu.SemaphoreType.DMA((2,))],
        compiler_params=pltpu.CompilerParams(vmem_limit_bytes=48 << 20),
        name="head_product",
    )(x, top, w)


def excess_kernel(stats_ref, own_ref, target_ref, draft_ref, excess_ref, mass_ref, ratio_ref):
    rows = target_ref.shape[0]
    stats = stats_ref[:, 0, :]

    def turn(values, lanes):
        return pltpu.roll(jnp.broadcast_to(values, (8, 128)), lanes % 128, 1)[:1]

    peak = jnp.max(stats, axis=0, keepdims=True)
    weights = pltpu.roll(jnp.exp(stats - peak), rows, 1)
    total = jnp.sum(stats * weights, axis=0, keepdims=True)
    pick = jnp.sum(stats, axis=0, keepdims=True)
    scale = turn(jnp.exp(own_ref[...] - peak), rows) / total
    log_prob = turn(pick, -2 * rows) - peak - jnp.log(turn(total, -rows))
    ratio_ref[...] = log_prob - turn(log_prob, -3 * rows)
    row = lax.broadcasted_iota(jnp.int32, (rows, 128), 0)
    lane = lax.broadcasted_iota(jnp.int32, (rows, 128), 1)

    def column(first):
        return jnp.sum(jnp.where(lane == row + first, scale, 0.0), axis=1, keepdims=True)

    excess = jnp.maximum(
        target_ref[...] * column(rows) - draft_ref[...] * column(4 * rows), 0.0
    )
    excess_ref[...] = excess
    mass = jnp.sum(excess, axis=1, keepdims=True)
    mass = jnp.sum(jnp.where(lane == row, mass, 0.0), axis=0, keepdims=True)
    mass_ref[...] = jnp.broadcast_to(mass[None], mass_ref.shape)


def excess_of(stats, own, exp_target, exp_draft):
    return pl.pallas_call(
        excess_kernel,
        out_shape=(
            jax.ShapeDtypeStruct(exp_target.shape, f32),
            jax.ShapeDtypeStruct(stats.shape, f32),
            jax.ShapeDtypeStruct(own.shape, f32),
        ),
        compiler_params=pltpu.CompilerParams(vmem_limit_bytes=4 << 20),
        name="excess",
    )(stats, own, exp_target, exp_draft)


def finish_kernel(vocab_total, excess_ref, mass_ref, ratio_ref, live_ref, rows_ref, accept_ref):
    row_count = excess_ref.shape[0]
    seq_count, span = accept_ref.shape
    position = lax.broadcasted_iota(jnp.int32, (1, 128), 1) % span
    live = position < live_ref[...]
    excess_mass = jnp.sum(mass_ref[...], axis=0)
    scale = jnp.where(live, vocab_total / (excess_mass + 1e-06), 0.0)
    row = lax.broadcasted_iota(jnp.int32, (row_count, 128), 0)
    lane = lax.broadcasted_iota(jnp.int32, (row_count, 128), 1)
    column = jnp.sum(jnp.where(row == lane, scale, 0.0), axis=1, keepdims=True)
    rows_ref[...] = excess_ref[...] * column
    steps = jnp.where(live, jnp.minimum(ratio_ref[...], 0.0), 0.0)
    row = lax.broadcasted_iota(jnp.int32, (seq_count, 128), 0)
    lane = lax.broadcasted_iota(jnp.int32, (seq_count, 128), 1)
    total = jnp.zeros((seq_count, 1), f32)
    for k in range(span):
        at = lane == row * span + k
        total = total + jnp.sum(jnp.where(at, steps, 0.0), axis=1, keepdims=True)
        alive = jnp.sum(jnp.where(at & live, 1.0, 0.0), axis=1, keepdims=True)
        accept_ref[:, k : k + 1] = jnp.where(alive > 0.0, total, 0.0)


def finish(excess, mass, log_ratio, live_rows, vocab_total, seq_count, span):
    return pl.pallas_call(
        functools.partial(finish_kernel, float(vocab_total)),
        out_shape=(
            jax.ShapeDtypeStruct(excess.shape, f32),
            jax.ShapeDtypeStruct((seq_count, span), f32),
        ),
        compiler_params=pltpu.CompilerParams(vmem_limit_bytes=4 << 20),
        name="finish",
    )(excess, mass, log_ratio, live_rows)


def per_device(partials, residual, norm_gain, head_weight, draft_logits, draft_tokens, live_drafts):
    dps = lax.axis_size("dp")
    sections = lax.axis_size("section")
    cores = lax.axis_size("core")
    owners = lax.axis_size(tensor_axes)
    chips = owners // cores
    tensor_at = lax.axis_index(tensor_axes)
    core_at = lax.axis_index("core")
    rows, width = residual.shape
    feature_count = width * sections
    own_rows = rows // owners
    depth, vocab_slice = head_weight.shape
    seq_count, draft_span = draft_tokens.shape
    row_count = seq_count * draft_span

    draft_block = draft_logits[0, 0, 0]
    source_rows, draft_width = draft_block.shape
    group_size = draft_width // vocab_slice
    member = tensor_at % group_size

    def draft_piece(block, flip):
        return lax.dynamic_slice_in_dim(block, (member ^ flip) * vocab_slice, vocab_slice, 1)

    terms = partials[0]
    half = rows // cores
    kept = lax.dynamic_slice_in_dim(terms, core_at * half, half, 0)
    given = lax.dynamic_slice_in_dim(terms, (1 - core_at) * half, half, 0)
    beside = draft_piece(draft_block, 1)
    beside = jnp.pad(beside, ((0, 8 - source_rows), (0, width - vocab_slice)))
    got = lax.ppermute(
        jnp.concatenate([given, beside]), "core", [(i, cores - 1 - i) for i in range(cores)]
    )
    own_at = (core_at * chips + lax.axis_index("zy")) * own_rows
    own_residual = lax.dynamic_slice_in_dim(residual, own_at, own_rows, 0)
    lanes = width // 8
    own_residual = own_residual.reshape(own_rows, 8, lanes).astype(f32)
    gain = norm_gain.reshape(8, lanes).astype(f32)
    got, kept, own_residual, gain, draft_block, head_weight = lax.optimization_barrier(
        (got, kept, own_residual, gain, draft_block, head_weight)
    )
    arrived = [draft_piece(draft_block, 0), got[half : half + source_rows, :vocab_slice]]
    got = got[:half]
    pair = ((kept.astype(f32) + got.astype(f32)) * pair_scale).astype(f16)
    pair_sums = exchange(pair.reshape(chips, own_rows, 8, lanes), "zy")
    for flip in range(2, group_size):
        arrived.append(
            lax.ppermute(
                draft_piece(draft_block, flip), tensor_axes, [(i, i ^ flip) for i in range(owners)]
            )
        )
    arrived = jnp.stack(arrived)
    pair_sums, weight_top = lax.optimization_barrier((pair_sums, head_weight[: depth // 2]))
    layer_total = jnp.sum(pair_sums.astype(f32), axis=0) * (1.0 / pair_scale)

    hidden = lax.reduce_precision(own_residual + layer_total, 8, 7)
    squares = lax.psum(jnp.sum(hidden * hidden, axis=(1, 2)), "section")
    factor = lax.rsqrt(squares / feature_count + norm_epsilon)
    normed_own = (hidden * factor[:, None, None] * gain[None]).astype(bf16)

    normed_own, arrived, draft_tokens, live_drafts, core_at, tensor_at, member = (
        lax.optimization_barrier(
            (normed_own, arrived, draft_tokens, live_drafts, core_at, tensor_at, member)
        )
    )

    by_block = jnp.transpose(normed_own.reshape(own_rows, dps, depth), (1, 0, 2))
    to_send = jnp.broadcast_to(by_block[:, None], (dps, chips, own_rows, depth))
    mine = exchange(to_send.reshape(dps * chips, own_rows, depth), ("dp", "zy"))
    mine = mine.reshape(dps, rows // cores, depth)
    mine, arrived, draft_tokens, live_drafts, core_at, tensor_at, member = (
        lax.optimization_barrier(
            (mine, arrived, draft_tokens, live_drafts, core_at, tensor_at, member)
        )
    )
    other = lax.ppermute(mine, "core", [(0, 1), (1, 0)])

    drafted = jnp.concatenate(
        [
            lax.dynamic_index_in_dim(arrived, member ^ source, 0, keepdims=False)
            for source in range(group_size)
        ]
    ).astype(f32)
    local_ids = draft_tokens.reshape(row_count) - tensor_at * vocab_slice
    live_rows = one_row(jnp.repeat(live_drafts, draft_span))

    def statistics(values):
        peak = jnp.max(values, axis=1)
        exps = jnp.exp(values - peak[:, None])
        chosen = lax.broadcasted_iota(jnp.int32, values.shape, 1) == local_ids[:, None]
        pick = jnp.sum(jnp.where(chosen, values, 0.0), axis=1)
        return exps, [peak, jnp.sum(exps, axis=1), pick]

    exp_draft, stats_draft = statistics(drafted)
    other, exp_draft, stats_draft, live_rows, local_ids = lax.optimization_barrier(
        (other, exp_draft, stats_draft, live_rows, local_ids)
    )

    normed = jnp.where(
        core_at == 0, jnp.stack([mine, other], axis=1), jnp.stack([other, mine], axis=1)
    ).reshape(dps * rows, depth)
    products = head_product(normed, weight_top, head_weight)
    products = (products * block_scale).astype(f16)

    by_dp = exchange(products, "dp").reshape(dps, rows, vocab_slice)

    by_dp = (jnp.sum(by_dp.astype(f32), axis=0) * (dp_scale / block_scale)).astype(f16)
    gathered = exchange(by_dp, "section").reshape(sections, row_count, vocab_slice)
    logits = jnp.sum(gathered.astype(f32), axis=0) * (1.0 / dp_scale)

    exp_target, stats_target = statistics(logits)
    own = one_row(jnp.concatenate(stats_target + stats_draft))
    stats = exchange(jnp.broadcast_to(own[None], (owners, 1, 128)), share_axes)
    excess, mass, log_ratio = excess_of(stats, own, exp_target, exp_draft)
    mass = exchange(mass, share_axes)
    return finish(
        excess, mass, log_ratio, live_rows, vocab_slice * owners, seq_count, draft_span
    )


def solution(mesh):
    sizes = mesh.shape
    split = Mesh(
        mesh.devices.reshape(sizes["dp"], sizes["tensor"] // 2, 2, sizes["section"]),
        ("dp",) + tensor_axes + ("section",),
    )
    return jax.shard_map(
        per_device,
        mesh=split,
        in_specs=(
            P(tensor_axes, "dp", "section"),
            P("dp", "section"),
            P("section"),
            P(("section", "dp"), tensor_axes),
            P("dp", "section", tensor_axes, None, None),
            P(("dp", "section"), None),
            P(("dp", "section")),
        ),
        out_specs=(P(("dp", "section"), tensor_axes), P(("dp", "section"), None)),
        check_vma=False,
    )
```
